32 devices in a mesh: mask: 4 (over z), rows: 8 (over y, x, core).
Axes of the slice: x: 2, y: 2, z: 4, core: 2. Of those that a mesh axis runs over, the one named last changes fastest.
Arguments:
- object_field: float32 [2, 4096, 4096], P(None, 'rows'), may hold values from -6 to 6
- phases: int32 [4, 4096, 4096], P('mask', 'rows'), may hold values from 0 to 3
- intensity: float32 [4, 4096, 4096], P('mask', 'rows'), may hold values from 0.5 to 4
Outputs:
- updated: float32 [2, 4096, 4096], P(None, 'rows')
- gradient: float32 [2, 4096, 4096], P(None, 'rows')
The draws below stay inside these ranges and needn't reach their ends.
Inputs may be any that keep to these rules, and one draw needn't show every extreme that they name: `phases`: index k stands for the mask entry i^k.
All inputs are finite; a program needn't handle non-finite values.
Results may differ from the reference program's by a relative error of at most 0.00011.
Values sent between devices are 32-bit elements; how exact they have to be, the bound alone decides.
A program may use at most 192 MiB of HBM per device.

```python
import math
import jax
import jax.numpy as jnp
from jax import lax

N = 4096
L = 4


def set_ends(entries, stream_key, least, largest):
    longest = entries.shape.index(max(entries.shape))
    spots = []
    for shift in (0, 1):
        where = [jax.random.randint(jax.random.fold_in(stream_key, axis), (), 0, length) for axis, length in enumerate(entries.shape)]
        where[longest] = (where[longest] + shift) % entries.shape[longest]
        spots.append(tuple(where))
    return entries.at[spots[0]].set(least).at[spots[1]].set(largest)


def levels(key, extent, pieces, smallest, largest):
    loudness = 1.0
    for dim, shards_of in pieces:
        heights = jax.random.uniform(jax.random.fold_in(jax.random.fold_in(key, 6), dim), (shards_of,), jnp.float32, smallest / len(pieces), largest / len(pieces))
        loudness = loudness * jnp.repeat(jnp.exp(heights), extent[dim] // shards_of).reshape((-1,) + (1,) * (len(extent) - 1 - dim))
    return loudness


def gaussian(own_key, extent, spread, bound, shards=(), kind=jnp.bfloat16):
    values = spread * jax.random.normal(own_key, extent, jnp.float32)
    if shards:
        values = values * levels(own_key, extent, shards, -0.22, 0.18)
    return jnp.clip(values, -bound, bound).astype(kind)


def setup_inputs(seed: int = 0) -> dict:
    keys = jax.random.split(jax.random.key(seed), 4)
    return {
        "object_field": gaussian(keys[0], (2, N, N), 1.0, 6.0, ((1, 8),), jnp.float32),
        "phases": set_ends(jax.random.randint(keys[1], (L, N, N), 0, 4), jax.random.fold_in(keys[1], 1), 0, 3).astype(jnp.int32),
        "intensity": jnp.clip(jnp.exp(math.log(4.0) - 2.0794415 * jax.random.uniform(keys[2], (L, N, N), jnp.float32) ** levels(keys[2], (L, N, N), ((0, 4), (1, 8)), -0.2, 0.2)), 0.5, 4.0),
    }


def reference(object_field, phases, intensity):
    zc = lax.complex(object_field[0], object_field[1])
    grad = jnp.zeros_like(zc)
    for index in range(L):
        code = phases[index]
        d_real = (jnp.where(code == 0, 1.0, 0.0) - jnp.where(code == 2, 1.0, 0.0)).astype(object_field.dtype)
        d_imag = (jnp.where(code == 1, 1.0, 0.0) - jnp.where(code == 3, 1.0, 0.0)).astype(object_field.dtype)
        mask_val = lax.complex(d_real, d_imag)
        wave = jnp.fft.fft2(mask_val * zc, norm="ortho")
        weight = jnp.abs(wave) ** 2 - intensity[index].T
        back = jnp.fft.ifft2(weight * wave, norm="ortho")
        grad = grad + jnp.conj(mask_val) * back
    direction = (1.0 / L) * grad
    updated = zc - 0.2 * direction
    updated_out = jnp.stack([jnp.real(updated), jnp.imag(updated)]).astype(object_field.dtype)
    gradient_out = jnp.stack([jnp.real(direction), jnp.imag(direction)]).astype(object_field.dtype)
    return (updated_out, gradient_out)
```

```python
import math

import jax
import jax.numpy as jnp
import ml_dtypes
import numpy as np
from jax import lax
from jax.experimental import pallas as pl
from jax.experimental.pallas import tpu as pltpu
from jax.sharding import PartitionSpec as P

P_SIZE = 32
Q = 128


step_size = 0.2


def dft_table(length, sign):
    idx = jnp.arange(length, dtype=jnp.int32)
    expo = idx[:, None] * idx[None, :] % length
    angle = expo.astype(jnp.float32) * (sign * 2.0 * math.pi / length)
    return (jnp.cos(angle), jnp.sin(angle))


def twiddle_table(first, second, sign):
    left = jnp.arange(first, dtype=jnp.int32)
    right = jnp.arange(second, dtype=jnp.int32)
    total = first * second
    expo = left[:, None] * right[None, :] % total
    angle = expo.astype(jnp.float32) * (sign * 2.0 * math.pi / total)
    return (jnp.cos(angle), jnp.sin(angle))


def stacked_table(t_real, t_imag):
    upper = jnp.stack([t_real, t_imag], axis=1)
    lower = jnp.stack([-t_imag, t_real], axis=1)
    return jnp.stack([upper, lower])


def contract(form, left, right):
    return jnp.einsum(
        form, left, right, precision=lax.Precision.HIGHEST, preferred_element_type=jnp.float32
    )


def along_last(stacked, sign, flip):
    lead = stacked.shape[1]
    length = P_SIZE * Q
    p_real, p_imag = dft_table(P_SIZE, sign)
    q_real, q_imag = dft_table(Q, sign)
    t_real, t_imag = twiddle_table(P_SIZE, Q, sign)
    factor = 1.0 / math.sqrt(length)
    first_table = stacked_table(p_real, p_imag)
    second_table = stacked_table(q_real * factor, q_imag * factor)
    inner = contract("cbpq,cpek->ebkq", stacked.reshape(2, lead, P_SIZE, Q), first_table)
    b_real = inner[0] * t_real - inner[1] * t_imag
    b_imag = inner[0] * t_imag + inner[1] * t_real
    twisted = jnp.stack([b_real, b_imag])
    if flip:
        return contract("cbkq,cqem->emkb", twisted, second_table).reshape(2, length, lead)
    return contract("cbkq,cqem->ebmk", twisted, second_table).reshape(2, lead, length)


def plain_body(object_field, phases, intensity):
    groups = lax.axis_size("rows")
    masks = lax.axis_size("mask")
    own_rows = object_field.shape[1]
    length = object_field.shape[2]
    own_cols = length // groups
    code = phases[0]
    d_real = jnp.where(code == 0, 1.0, 0.0) - jnp.where(code == 2, 1.0, 0.0)
    d_imag = jnp.where(code == 1, 1.0, 0.0) - jnp.where(code == 3, 1.0, 0.0)
    z_real = object_field[0]
    z_imag = object_field[1]
    coded = jnp.stack([d_real * z_real - d_imag * z_imag, d_real * z_imag + d_imag * z_real])
    result = along_last(coded, -1.0, True)
    received = lax.all_to_all(
        result.reshape(2, groups, own_cols, own_rows),
        "rows",
        split_axis=1,
        concat_axis=1,
        tiled=True,
    )
    columns = jnp.transpose(received, (0, 2, 1, 3)).reshape(2, own_cols, length)
    wave = along_last(columns, -1.0, False)
    weight = wave[0] * wave[0] + wave[1] * wave[1] - intensity[0]
    weighted = along_last(wave * weight[None], 1.0, False)
    outgoing = weighted.reshape(2, own_cols, groups, own_rows)
    returned = lax.all_to_all(outgoing, "rows", split_axis=2, concat_axis=2, tiled=True)
    panel = jnp.transpose(returned, (0, 3, 2, 1)).reshape(2, own_rows, length)
    back = along_last(panel, 1.0, False)
    g_real = back[0]
    g_imag = back[1]
    term = jnp.stack([d_real * g_real + d_imag * g_imag, d_real * g_imag - d_imag * g_real])
    inverse_count = 1.0 / masks
    total = lax.psum(term, "mask")
    direction = inverse_count * total
    return (object_field - step_size * direction, direction)


LANES = 128


def host_tables(sign, scale):
    idx = np.arange(Q)
    angle = sign * 2.0 * np.pi * ((idx[:, None] * idx[None, :]) % Q) / Q
    cos, sin = np.cos(angle) * scale, np.sin(angle) * scale
    table = np.block([[cos, sin], [-sin, cos]]).astype(np.float32)
    high = table.astype(ml_dtypes.bfloat16)
    low = (table - high.astype(np.float32)).astype(ml_dtypes.bfloat16)
    return high, low


def host_twiddle(sign):
    expo = np.arange(P_SIZE)[:, None] * np.arange(Q)[None, :]
    angle = sign * 2.0 * np.pi * expo / (P_SIZE * Q)
    return np.stack([np.cos(angle), np.sin(angle)]).astype(np.float32)


def butterflies(real, imag, sign):
    count = len(real)
    if count == 1:
        return real, imag
    e_real, e_imag = butterflies(real[0::2], imag[0::2], sign)
    o_real, o_imag = butterflies(real[1::2], imag[1::2], sign)
    half = count // 2
    out_real, out_imag = [None] * count, [None] * count
    for k in range(half):
        a, b = o_real[k], o_imag[k]
        if k == 0:
            t_real, t_imag = a, b
        elif 4 * k == count:
            t_real, t_imag = (b, -a) if sign < 0 else (-b, a)
        elif 8 * k == count:
            root = math.sqrt(0.5)
            if sign < 0:
                t_real, t_imag = (a + b) * root, (b - a) * root
            else:
                t_real, t_imag = (a - b) * root, (a + b) * root
        elif 8 * k == 3 * count:
            root = math.sqrt(0.5)
            if sign < 0:
                t_real, t_imag = (b - a) * root, (a + b) * -root
            else:
                t_real, t_imag = (a + b) * -root, (a - b) * root
        else:
            angle = sign * 2.0 * math.pi * k / count
            c, s = math.cos(angle), math.sin(angle)
            t_real, t_imag = a * c - b * s, a * s + b * c
        out_real[k], out_imag[k] = e_real[k] + t_real, e_imag[k] + t_imag
        out_real[k + half], out_imag[k + half] = e_real[k] - t_real, e_imag[k] - t_imag
    return out_real, out_imag


def halves(value):
    high = value.astype(jnp.bfloat16)
    low = (value - high.astype(jnp.float32)).astype(jnp.bfloat16)
    return high, low


def dims_dot(left, right, dims):
    return lax.dot_general(left, right, (dims, ((), ())), preferred_element_type=jnp.float32)


def times_table(value, high_ref, low_ref):
    high, low = halves(value)
    dims = ((1,), (0,))
    total = dims_dot(high, high_ref[...], dims)
    total += dims_dot(low, high_ref[...], dims)
    return total + dims_dot(high, low_ref[...], dims)


def mask_entry(code):
    d_real = jnp.where(code == 0, 1.0, 0.0) - jnp.where(code == 2, 1.0, 0.0)
    d_imag = jnp.where(code == 1, 1.0, 0.0) - jnp.where(code == 3, 1.0, 0.0)
    return d_real, d_imag


def column_block(load, store, power_ref, power_rows, tw_refs, tables, mid_ref, share):
    twf_ref, twi_ref = tw_refs
    fh_ref, fl_ref, ih_ref, il_ref = tables
    for h in range(share // 8):
        real = [load(0, h, n1) for n1 in range(P_SIZE)]
        imag = [load(1, h, n1) for n1 in range(P_SIZE)]
        real, imag = butterflies(real, imag, -1.0)
        for k1 in range(P_SIZE):
            c, s = twf_ref[0, k1 : k1 + 1, :], twf_ref[1, k1 : k1 + 1, :]
            at = slice(k1 * share + h * 8, k1 * share + h * 8 + 8)
            mid_ref[at, 0:LANES] = real[k1] * c - imag[k1] * s
            mid_ref[at, LANES : 2 * LANES] = real[k1] * s + imag[k1] * c
    wave = times_table(mid_ref[...], fh_ref, fl_ref)
    w_real, w_imag = wave[:, 0:LANES], wave[:, LANES : 2 * LANES]
    weight = w_real * w_real + w_imag * w_imag - power_ref[power_rows, :]
    value = jnp.concatenate([w_real * weight, w_imag * weight], axis=1)
    mid_ref[...] = times_table(value, ih_ref, il_ref)
    for h in range(share // 8):
        real, imag = [], []
        for k1 in range(P_SIZE):
            c, s = twi_ref[0, k1 : k1 + 1, :], twi_ref[1, k1 : k1 + 1, :]
            at = slice(k1 * share + h * 8, k1 * share + h * 8 + 8)
            x, y = mid_ref[at, 0:LANES], mid_ref[at, LANES : 2 * LANES]
            real.append(x * c - y * s)
            imag.append(x * s + y * c)
        real, imag = butterflies(real, imag, 1.0)
        for n1 in range(P_SIZE):
            store(0, h, n1, real[n1])
            store(1, h, n1, imag[n1])


MESH = pl.DeviceIdType.MESH


def greet(peers):
    barrier = pltpu.get_barrier_semaphore()
    for peer in peers:
        pl.semaphore_signal(barrier, inc=1, device_id=peer, device_id_type=MESH)
    pl.semaphore_wait(barrier, len(peers))


def kernel_forward(
    z_hbm, code_hbm, power_hbm, twf_ref, twi_ref, ah_ref, al_ref, fh, fl, ih, il,
    u_hbm, buf, got, z_in, code_in, raw, turned, power, mid_ref,
    z_sem, code_sem, raw_sem, own_sem, out_sem, send_sem, recv_sem,
):
    _, halfs, _, groups, share, _ = buf.shape
    rows = z_in.shape[2]
    own = z_hbm.shape[1]
    batch = P_SIZE // send_sem.shape[0]
    per = rows // share
    me = lax.axis_index("rows")
    peers = [lax.rem(me + d, groups) for d in range(1, groups)]

    def load(i, slot):
        span = pl.ds(pl.multiple_of(i * rows, rows), rows)
        return (
            pltpu.make_async_copy(z_hbm.at[:, span], z_in.at[slot], z_sem.at[slot]),
            pltpu.make_async_copy(code_hbm.at[0, span], code_in.at[slot], code_sem.at[slot]),
        )

    def raw_load(o):
        slot = lax.rem(o, 2)
        span = pl.ds(pl.multiple_of(o * 8, 8), 8)
        return pltpu.make_async_copy(power_hbm.at[:, span], raw.at[slot], raw_sem.at[slot])

    octets = P_SIZE // 8

    for copy in load(0, 0):
        copy.start()
    raw_load(0).start()

    chunks = own // rows

    def first(i, carry):
        slot = lax.rem(i, 2)

        @pl.when(i + 1 < chunks)
        def _():
            for copy in load(i + 1, lax.rem(i + 1, 2)):
                copy.start()

        for copy in load(i, slot):
            copy.wait()

        def eight(g, carry):
            at = i * per + g // 2
            h, rest = at // (2 * groups), lax.rem(at, 2 * groups)
            part, c = rest // groups, lax.rem(rest, groups)
            sub = pl.ds(pl.multiple_of(lax.rem(g, 2) * 8, 8), 8)
            span = pl.ds(pl.multiple_of(g * 8, 8), 8)
            real, imag = [], []
            for n1 in range(P_SIZE):
                lanes = pl.ds(n1 * LANES, LANES)
                d_real, d_imag = mask_entry(code_in[slot, span, lanes])
                x, y = z_in[slot, 0, span, lanes], z_in[slot, 1, span, lanes]
                real.append(d_real * x - d_imag * y)
                imag.append(d_real * y + d_imag * x)
            real, imag = butterflies(real, imag, -1.0)
            for k1 in range(P_SIZE):
                cos, sin = twf_ref[0, k1 : k1 + 1, :], twf_ref[1, k1 : k1 + 1, :]
                buf[k1, h, part, c, sub, 0:LANES] = real[k1] * cos - imag[k1] * sin
                buf[k1, h, part, c, sub, LANES : 2 * LANES] = real[k1] * sin + imag[k1] * cos
            return carry

        return lax.fori_loop(0, rows // 8, eight, carry)

    lax.fori_loop(0, chunks, first, 0)
    greet([{"rows": peer} for peer in peers])

    def span_of(kg):
        return pl.ds(kg * batch, batch)

    def permute(o):
        raw_load(o).wait()

        @pl.when(o + 1 < octets)
        def _():
            raw_load(o + 1).start()

        slot = lax.rem(o, 2)

        def turn(i, carry):
            lanes = pl.ds(pl.multiple_of(i * LANES, LANES), LANES)
            block = raw[slot, :, :, lanes].reshape(Q, LANES)
            turned[pl.ds(pl.multiple_of(i * LANES, LANES), LANES), :] = block.T
            return carry

        lax.fori_loop(0, P_SIZE, turn, 0)

        def back(ak1, carry):
            block = turned[pl.ds(ak1, Q, stride=P_SIZE), :]
            power[o, pl.ds(pl.multiple_of(ak1 * Q, Q), Q), :] = block.T
            return carry

        lax.fori_loop(0, P_SIZE, back, 0)

    def own_copy(kg):
        span = span_of(kg)
        return pltpu.make_async_copy(buf.at[span, :, :, me], got.at[me, span], own_sem.at[kg])

    def send(kg, peer, sender):
        span = span_of(kg)
        return pltpu.make_async_remote_copy(
            src_ref=buf.at[span, :, :, peer],
            dst_ref=got.at[sender, span],
            send_sem=send_sem.at[kg, peer],
            recv_sem=recv_sem.at[kg, sender],
            device_id={"rows": peer},
            device_id_type=MESH,
        )

    def spread(kg):
        def one(j, carry):
            k1 = kg * batch + j
            for h in range(halfs):
                value = buf[k1, h].reshape(2 * Q, 2 * LANES)
                high, low = halves(value)
                dims = ((1,), (1,))
                total = dims_dot(ah_ref[...], high, dims)
                total += dims_dot(ah_ref[...], low, dims)
                total += dims_dot(al_ref[...], high, dims)
                buf[k1, h] = total.reshape(2, groups, share, 2 * LANES)
            return carry

        lax.fori_loop(0, batch, one, 0)
        own_copy(kg).start()
        for peer in peers:
            send(kg, peer, me).start()

    def gather(kg):
        own_copy(kg).wait()
        for peer in peers:
            send(kg, peer, peer).wait_recv()

        def one(j, carry):
            k1 = kg * batch + j
            strided = pl.ds(lax.rem(k1, 8), P_SIZE * share, stride=8)
            weights = power.at[k1 // 8]

            def where(part, h, n1):
                s, tile = n1 // (2 * halfs), n1 % (2 * halfs)
                lanes = pl.ds((tile % 2) * LANES, LANES)
                return s, k1, tile // 2, part, pl.ds(h * 8, 8), lanes

            def fetch(part, h, n1):
                return got[where(part, h, n1)]

            def store(part, h, n1, value):
                got[where(part, h, n1)] = value

            column_block(
                fetch, store, weights, strided, (twf_ref, twi_ref), (fh, fl, ih, il),
                mid_ref, share,
            )
            return carry

        lax.fori_loop(0, batch, one, 0)
        out_copy(kg).start()

    def out_copy(kg):
        span = span_of(kg)
        return pltpu.make_async_copy(got.at[:, span], u_hbm.at[:, span], out_sem.at[kg])

    count = send_sem.shape[0]
    lag = 2

    def turn(i, carry):
        @pl.when(i < count)
        def _():
            spread(i)

        @pl.when(jnp.logical_and(i < count, lax.rem(i * batch, 8) == 0))
        def _():
            permute(i * batch // 8)

        @pl.when(i >= lag)
        def _():
            gather(i - lag)

        return carry

    lax.fori_loop(0, count + lag, turn, 0)

    def finish(kg, carry):
        out_copy(kg).wait()
        for peer in peers:
            send(kg, peer, me).wait_send()
        return carry

    lax.fori_loop(0, count, finish, 0)


def kernel_backward(
    u_hbm, code_hbm, tw_ref, ih, il,
    total_hbm, land_a, land_b, buf, term, code_in, slot, stage,
    code_sem, own_sem, send_sem, recv_sem,
    a_send, a_recv, b_send, b_recv, s_send, s_recv, o_sem, slot_sem,
):
    _, _, _, groups, share, _ = buf.shape
    quarters = send_sem.shape[0]
    chunks, _, tall, _ = land_a.shape
    each = chunks // quarters
    ring = stage.shape[0]
    me, z = lax.axis_index("rows"), lax.axis_index("mask")
    masks = 4
    peers = [lax.rem(me + d, groups) for d in range(1, groups)]
    partner = z + 1 - 2 * lax.rem(z, 2)
    middle = 3 - z
    inner = jnp.logical_or(z == 1, z == 2)
    outer = jnp.logical_or(z == 0, z == 3)

    def place(q):
        return q // 2, pl.ds(pl.multiple_of(lax.rem(q, 2) * LANES, LANES), LANES)

    def own_copy(q):
        h, lanes = place(q)
        return pltpu.make_async_copy(
            u_hbm.at[me, :, h, :, :, lanes], buf.at[:, h, :, me, :, lanes], own_sem.at[q]
        )

    def send(q, peer, sender):
        h, lanes = place(q)
        return pltpu.make_async_remote_copy(
            src_ref=u_hbm.at[peer, :, h, :, :, lanes],
            dst_ref=buf.at[:, h, :, sender, :, lanes],
            send_sem=send_sem.at[q, peer],
            recv_sem=recv_sem.at[q, sender],
            device_id={"rows": peer},
            device_id_type=MESH,
        )

    def code_load(q):
        span = pl.ds(pl.multiple_of(q * LANES, LANES), LANES)
        return pltpu.make_async_copy(code_hbm.at[0, span], code_in.at[lax.rem(q, 2)], code_sem.at[q])

    def start(q):
        code_load(q).start()
        own_copy(q).start()
        for peer in peers:
            send(q, peer, me).start()

    def sent(q):
        for peer in peers:
            send(q, peer, me).wait_send()

    def invert(q):
        code_load(q).wait()
        own_copy(q).wait()
        for peer in peers:
            send(q, peer, peer).wait_recv()
        h, lanes = place(q)
        span = pl.ds(pl.multiple_of(q * LANES, LANES), LANES)

        def one(k1, carry):
            value = buf[k1, h, :, :, :, lanes].reshape(2 * Q, LANES)
            total = times_table(value.T, ih, il)
            cos, sin = tw_ref[0, pl.ds(k1, 1), :], tw_ref[1, pl.ds(k1, 1), :]
            x, y = total[:, 0:LANES], total[:, LANES : 2 * LANES]
            term[k1, span, 0:LANES] = x * cos - y * sin
            term[k1, span, LANES : 2 * LANES] = x * sin + y * cos
            return carry

        lax.fori_loop(0, P_SIZE, one, 0)

        def eight(g, carry):
            span = pl.ds(pl.multiple_of(q * LANES + g * 8, 8), 8)
            near = pl.ds(pl.multiple_of(g * 8, 8), 8)
            real = [term[k1, span, 0:LANES] for k1 in range(P_SIZE)]
            imag = [term[k1, span, LANES : 2 * LANES] for k1 in range(P_SIZE)]
            real, imag = butterflies(real, imag, 1.0)
            for n1 in range(P_SIZE):
                code = code_in[lax.rem(q, 2), near, pl.ds(n1 * LANES, LANES)]
                d_real, d_imag = mask_entry(code)
                term[n1, span, 0:LANES] = d_real * real[n1] + d_imag * imag[n1]
                term[n1, span, LANES : 2 * LANES] = d_real * imag[n1] - d_imag * real[n1]
            return carry

        lax.fori_loop(0, LANES // 8, eight, 0)

    def rows_of(j):
        return pl.ds(pl.multiple_of(j * tall, tall), tall)

    def hop(j, land, send_sems, recv_sems, target):
        return pltpu.make_async_remote_copy(
            src_ref=term.at[:, rows_of(j)],
            dst_ref=land.at[j],
            send_sem=send_sems.at[j],
            recv_sem=recv_sems.at[j],
            device_id={"mask": target},
            device_id_type=MESH,
        )

    def hop_a(j):
        return hop(j, land_a, a_send, a_recv, partner)

    def hop_b(j):
        return hop(j, land_b, b_send, b_recv, middle)

    def hop_s(j):
        return pltpu.make_async_remote_copy(
            src_ref=stage.at[lax.rem(j, ring)],
            dst_ref=total_hbm.at[:, rows_of(j)],
            send_sem=s_send.at[j],
            recv_sem=s_recv.at[j],
            device_id={"mask": partner},
            device_id_type=MESH,
        )

    def keep(j):
        return pltpu.make_async_copy(
            stage.at[lax.rem(j, ring)], total_hbm.at[:, rows_of(j)], o_sem.at[j]
        )

    def outer_step(j):
        @pl.when(j >= 2)
        def _():
            hop_a(j - 2).wait_send()

        hop_a(j).start()

    def inner_first(j):
        hop_a(j).wait_recv()
        copy = pltpu.make_async_copy(land_a.at[j], slot.at[0], slot_sem.at[0])
        copy.start()
        copy.wait()

        def add(n1, carry):
            term[n1, rows_of(j)] = term[n1, rows_of(j)] + slot[0, n1]
            return carry

        lax.fori_loop(0, P_SIZE, add, 0)
        hop_b(j).start()

    def inner_second(j):
        hop_b(j).wait_recv()
        copy = pltpu.make_async_copy(land_b.at[j], slot.at[1], slot_sem.at[1])
        copy.start()

        @pl.when(j >= ring)
        def _():
            hop_s(j - ring).wait_send()
            keep(j - ring).wait()

        copy.wait()
        r = lax.rem(j, ring)
        for n1 in range(P_SIZE):
            lanes = pl.ds(n1 * LANES, LANES)
            total = term[n1, rows_of(j)] + slot[1, n1]
            stage[r, 0, :, lanes] = total[:, 0:LANES]
            stage[r, 1, :, lanes] = total[:, LANES : 2 * LANES]
        hop_s(j).start()
        keep(j).start()

    greet(
        [{"rows": peer} for peer in peers]
        + [{"mask": lax.rem(z + d, masks)} for d in range(1, masks)]
    )
    start(0)
    sent(0)
    start(1)

    def turn(j, carry):
        q = j // each

        @pl.when(lax.rem(j, each) == 0)
        def _():
            invert(q)

        @pl.when(jnp.logical_and(lax.rem(j, each) == each // 2, q + 2 < quarters))
        def _():
            sent(q + 1)
            start(q + 2)

        @pl.when(outer)
        def _():
            outer_step(j)

        @pl.when(inner)
        def _():
            inner_first(j)

            @pl.when(j >= 1)
            def _():
                inner_second(j - 1)

        return carry

    lax.fori_loop(0, chunks, turn, 0)

    @pl.when(outer)
    def _():
        hop_a(chunks - 2).wait_send()
        hop_a(chunks - 1).wait_send()

        def arrive(j, carry):
            hop_s(j).wait_recv()
            return carry

        lax.fori_loop(0, chunks, arrive, 0)

    @pl.when(inner)
    def _():
        inner_second(chunks - 1)

        def leave(j, carry):
            hop_b(j).wait_send()
            return carry

        lax.fori_loop(0, chunks, leave, 0)

        def last(j, carry):
            hop_s(j).wait_send()
            keep(j).wait()
            return carry

        lax.fori_loop(chunks - ring, chunks, last, 0)

    sent(quarters - 1)


def fast_body(object_field, phases, intensity):
    groups = lax.axis_size("rows")
    masks = lax.axis_size("mask")
    own = object_field.shape[1]
    length = object_field.shape[2]
    share = Q // groups
    half_scale = 1.0 / math.sqrt(length)
    f_high, f_low = host_tables(-1.0, half_scale)
    i_high, i_low = host_tables(1.0, half_scale)
    tw_f, tw_i = host_twiddle(-1.0), host_twiddle(1.0)
    wide = 2 * Q
    f32 = jnp.float32
    vmem = pl.BlockSpec(memory_space=pltpu.VMEM)
    hbm = pl.BlockSpec(memory_space=pl.ANY)
    dma = pltpu.SemaphoreType.DMA

    power = intensity[0].reshape(share, P_SIZE, length)

    parts, rows, halfs = 8, 32, own // wide
    panel = (groups, P_SIZE, halfs, 2, share, wide)
    u = pl.pallas_call(
        kernel_forward,
        in_specs=[hbm] * 3 + [vmem] * 8,
        out_specs=hbm,
        out_shape=jax.ShapeDtypeStruct(panel, f32),
        scratch_shapes=[
            pltpu.VMEM((P_SIZE, halfs, 2, groups, share, wide), f32),
            pltpu.VMEM(panel, f32),
            pltpu.VMEM((2, 2, rows, length), f32),
            pltpu.VMEM((2, rows, length), jnp.int32),
            pltpu.VMEM((2, share, 8, length), f32),
            pltpu.VMEM((length, 8 * share), f32),
            pltpu.VMEM((P_SIZE // 8, length, Q), f32),
            pltpu.VMEM((P_SIZE * share, wide), f32),
            dma((2,)),
            dma((2,)),
            dma((2,)),
            dma((parts,)),
            dma((parts,)),
            dma((parts, groups)),
            dma((parts, groups)),
        ],
        compiler_params=pltpu.CompilerParams(
            collective_id=0, has_side_effects=True, vmem_limit_bytes=58 * 2**20
        ),
        name="forward_and_columns",
    )(object_field, phases, power, tw_f, tw_i, f_high.T, f_low.T, f_high, f_low, i_high, i_low)

    quarters, tall, ring = own // LANES, 16, 4
    chunks = own // tall
    landing = jax.ShapeDtypeStruct((chunks, P_SIZE, tall, wide), f32)
    total, _, _ = pl.pallas_call(
        kernel_backward,
        in_specs=[hbm] * 2 + [vmem] * 3,
        out_specs=[hbm] * 3,
        out_shape=[jax.ShapeDtypeStruct((2, own, length), f32), landing, landing],
        scratch_shapes=[
            pltpu.VMEM((P_SIZE, halfs, 2, groups, share, wide), f32),
            pltpu.VMEM((P_SIZE, own, wide), f32),
            pltpu.VMEM((2, LANES, length), jnp.int32),
            pltpu.VMEM((2, P_SIZE, tall, wide), f32),
            pltpu.VMEM((ring, 2, tall, length), f32),
            dma((quarters,)),
            dma((quarters,)),
            dma((quarters, groups)),
            dma((quarters, groups)),
        ]
        + [dma((chunks,))] * 7
        + [dma((2,))],
        compiler_params=pltpu.CompilerParams(
            collective_id=1, has_side_effects=True, vmem_limit_bytes=58 * 2**20
        ),
        name="back_and_sum",
    )(u, phases, tw_i, i_high, i_low)
    direction = total * (1.0 / masks)
    return (object_field - step_size * direction, direction)


def solution(mesh):
    def body(object_field, phases, intensity):
        groups = lax.axis_size("rows")
        masks = lax.axis_size("mask")
        own, length = object_field.shape[1:]
        fits = own % LANES == 0 and length == P_SIZE * Q and groups == 8 and masks == 4 and own % 256 == 0
        run = fast_body if fits else plain_body
        return run(object_field, phases, intensity)

    return jax.shard_map(
        body,
        mesh=mesh,
        in_specs=(P(None, "rows", None), P("mask", "rows", None), P("mask", "rows", None)),
        out_specs=(P(None, "rows", None), P(None, "rows", None)),
        check_vma=False,
    )
```

```python
import math

import jax
import jax.numpy as jnp
import ml_dtypes
import numpy as np
from jax import lax
from jax.experimental import pallas as pl
from jax.experimental.pallas import tpu as pltpu
from jax.sharding import PartitionSpec as P

P_SIZE = 32
Q = 128


step_size = 0.2


def dft_table(length, sign):
    idx = jnp.arange(length, dtype=jnp.int32)
    expo = idx[:, None] * idx[None, :] % length
    angle = expo.astype(jnp.float32) * (sign * 2.0 * math.pi / length)
    return (jnp.cos(angle), jnp.sin(angle))


def twiddle_table(first, second, sign):
    left = jnp.arange(first, dtype=jnp.int32)
    right = jnp.arange(second, dtype=jnp.int32)
    total = first * second
    expo = left[:, None] * right[None, :] % total
    angle = expo.astype(jnp.float32) * (sign * 2.0 * math.pi / total)
    return (jnp.cos(angle), jnp.sin(angle))


def stacked_table(t_real, t_imag):
    upper = jnp.stack([t_real, t_imag], axis=1)
    lower = jnp.stack([-t_imag, t_real], axis=1)
    return jnp.stack([upper, lower])


def contract(form, left, right):
    return jnp.einsum(
        form, left, right, precision=lax.Precision.HIGHEST, preferred_element_type=jnp.float32
    )


def along_last(stacked, sign, flip):
    lead = stacked.shape[1]
    length = P_SIZE * Q
    p_real, p_imag = dft_table(P_SIZE, sign)
    q_real, q_imag = dft_table(Q, sign)
    t_real, t_imag = twiddle_table(P_SIZE, Q, sign)
    factor = 1.0 / math.sqrt(length)
    first_table = stacked_table(p_real, p_imag)
    second_table = stacked_table(q_real * factor, q_imag * factor)
    inner = contract("cbpq,cpek->ebkq", stacked.reshape(2, lead, P_SIZE, Q), first_table)
    b_real = inner[0] * t_real - inner[1] * t_imag
    b_imag = inner[0] * t_imag + inner[1] * t_real
    twisted = jnp.stack([b_real, b_imag])
    if flip:
        return contract("cbkq,cqem->emkb", twisted, second_table).reshape(2, length, lead)
    return contract("cbkq,cqem->ebmk", twisted, second_table).reshape(2, lead, length)


def plain_body(object_field, phases, intensity):
    groups = lax.axis_size("rows")
    masks = lax.axis_size("mask")
    own_rows = object_field.shape[1]
    length = object_field.shape[2]
    own_cols = length // groups
    code = phases[0]
    d_real = jnp.where(code == 0, 1.0, 0.0) - jnp.where(code == 2, 1.0, 0.0)
    d_imag = jnp.where(code == 1, 1.0, 0.0) - jnp.where(code == 3, 1.0, 0.0)
    z_real = object_field[0]
    z_imag = object_field[1]
    coded = jnp.stack([d_real * z_real - d_imag * z_imag, d_real * z_imag + d_imag * z_real])
    result = along_last(coded, -1.0, True)
    received = lax.all_to_all(
        result.reshape(2, groups, own_cols, own_rows),
        "rows",
        split_axis=1,
        concat_axis=1,
        tiled=True,
    )
    columns = jnp.transpose(received, (0, 2, 1, 3)).reshape(2, own_cols, length)
    wave = along_last(columns, -1.0, False)
    weight = wave[0] * wave[0] + wave[1] * wave[1] - intensity[0]
    weighted = along_last(wave * weight[None], 1.0, False)
    outgoing = weighted.reshape(2, own_cols, groups, own_rows)
    returned = lax.all_to_all(outgoing, "rows", split_axis=2, concat_axis=2, tiled=True)
    panel = jnp.transpose(returned, (0, 3, 2, 1)).reshape(2, own_rows, length)
    back = along_last(panel, 1.0, False)
    g_real = back[0]
    g_imag = back[1]
    term = jnp.stack([d_real * g_real + d_imag * g_imag, d_real * g_imag - d_imag * g_real])
    inverse_count = 1.0 / masks
    total = lax.psum(term, "mask")
    direction = inverse_count * total
    return (object_field - step_size * direction, direction)


LANES = 128


def host_tables(sign, scale):
    idx = np.arange(Q)
    angle = sign * 2.0 * np.pi * ((idx[:, None] * idx[None, :]) % Q) / Q
    cos, sin = np.cos(angle) * scale, np.sin(angle) * scale
    table = np.block([[cos, sin], [-sin, cos]]).astype(np.float32)
    high = table.astype(ml_dtypes.bfloat16)
    low = (table - high.astype(np.float32)).astype(ml_dtypes.bfloat16)
    return high, low


def host_twiddle(sign):
    expo = np.arange(P_SIZE)[:, None] * np.arange(Q)[None, :]
    angle = sign * 2.0 * np.pi * expo / (P_SIZE * Q)
    return np.stack([np.cos(angle), np.sin(angle)]).astype(np.float32)


def butterflies(real, imag, sign):
    count = len(real)
    if count == 1:
        return real, imag
    e_real, e_imag = butterflies(real[0::2], imag[0::2], sign)
    o_real, o_imag = butterflies(real[1::2], imag[1::2], sign)
    half = count // 2
    out_real, out_imag = [None] * count, [None] * count
    for k in range(half):
        a, b = o_real[k], o_imag[k]
        if k == 0:
            t_real, t_imag = a, b
        elif 4 * k == count:
            t_real, t_imag = (b, -a) if sign < 0 else (-b, a)
        elif 8 * k == count:
            root = math.sqrt(0.5)
            if sign < 0:
                t_real, t_imag = (a + b) * root, (b - a) * root
            else:
                t_real, t_imag = (a - b) * root, (a + b) * root
        elif 8 * k == 3 * count:
            root = math.sqrt(0.5)
            if sign < 0:
                t_real, t_imag = (b - a) * root, (a + b) * -root
            else:
                t_real, t_imag = (a + b) * -root, (a - b) * root
        else:
            angle = sign * 2.0 * math.pi * k / count
            c, s = math.cos(angle), math.sin(angle)
            t_real, t_imag = a * c - b * s, a * s + b * c
        out_real[k], out_imag[k] = e_real[k] + t_real, e_imag[k] + t_imag
        out_real[k + half], out_imag[k + half] = e_real[k] - t_real, e_imag[k] - t_imag
    return out_real, out_imag


def halves(value):
    high = value.astype(jnp.bfloat16)
    low = (value - high.astype(jnp.float32)).astype(jnp.bfloat16)
    return high, low


def dims_dot(left, right, dims):
    return lax.dot_general(left, right, (dims, ((), ())), preferred_element_type=jnp.float32)


def times_table(value, high_ref, low_ref):
    high, low = halves(value)
    dims = ((1,), (0,))
    total = dims_dot(high, high_ref[...], dims)
    total += dims_dot(low, high_ref[...], dims)
    return total + dims_dot(high, low_ref[...], dims)


def mask_entry(code):
    d_real = jnp.where(code == 0, 1.0, 0.0) - jnp.where(code == 2, 1.0, 0.0)
    d_imag = jnp.where(code == 1, 1.0, 0.0) - jnp.where(code == 3, 1.0, 0.0)
    return d_real, d_imag


def column_block(load, store, power_ref, power_rows, tw_refs, tables, mid_ref, share):
    twf_ref, twi_ref = tw_refs
    fh_ref, fl_ref, ih_ref, il_ref = tables
    for h in range(share // 8):
        real = [load(0, h, n1) for n1 in range(P_SIZE)]
        imag = [load(1, h, n1) for n1 in range(P_SIZE)]
        real, imag = butterflies(real, imag, -1.0)
        for k1 in range(P_SIZE):
            c, s = twf_ref[0, k1 : k1 + 1, :], twf_ref[1, k1 : k1 + 1, :]
            at = slice(k1 * share + h * 8, k1 * share + h * 8 + 8)
            mid_ref[at, 0:LANES] = real[k1] * c - imag[k1] * s
            mid_ref[at, LANES : 2 * LANES] = real[k1] * s + imag[k1] * c
    wave = times_table(mid_ref[...], fh_ref, fl_ref)
    w_real, w_imag = wave[:, 0:LANES], wave[:, LANES : 2 * LANES]
    weight = w_real * w_real + w_imag * w_imag - power_ref[power_rows, :]
    value = jnp.concatenate([w_real * weight, w_imag * weight], axis=1)
    mid_ref[...] = times_table(value, ih_ref, il_ref)
    for h in range(share // 8):
        real, imag = [], []
        for k1 in range(P_SIZE):
            c, s = twi_ref[0, k1 : k1 + 1, :], twi_ref[1, k1 : k1 + 1, :]
            at = slice(k1 * share + h * 8, k1 * share + h * 8 + 8)
            x, y = mid_ref[at, 0:LANES], mid_ref[at, LANES : 2 * LANES]
            real.append(x * c - y * s)
            imag.append(x * s + y * c)
        real, imag = butterflies(real, imag, 1.0)
        for n1 in range(P_SIZE):
            store(0, h, n1, real[n1])
            store(1, h, n1, imag[n1])


MESH = pl.DeviceIdType.MESH


def greet(peers):
    barrier = pltpu.get_barrier_semaphore()
    for peer in peers:
        pl.semaphore_signal(barrier, inc=1, device_id=peer, device_id_type=MESH)
    pl.semaphore_wait(barrier, len(peers))


def kernel_forward(
    z_hbm, code_hbm, power_hbm, twf_ref, twi_ref, ah_ref, al_ref, fh, fl, ih, il,
    u_hbm, buf, got, z_in, code_in, raw, turned, power, mid_ref,
    z_sem, code_sem, raw_sem, own_sem, out_sem, send_sem, recv_sem,
):
    _, halfs, _, groups, share, _ = buf.shape
    rows = z_in.shape[2]
    own = z_hbm.shape[1]
    batch = P_SIZE // send_sem.shape[0]
    per = rows // share
    me = lax.axis_index("rows")
    peers = [lax.rem(me + d, groups) for d in range(1, groups)]

    def load(i, slot):
        span = pl.ds(pl.multiple_of(i * rows, rows), rows)
        return (
            pltpu.make_async_copy(z_hbm.at[:, span], z_in.at[slot], z_sem.at[slot]),
            pltpu.make_async_copy(code_hbm.at[0, span], code_in.at[slot], code_sem.at[slot]),
        )

    def raw_load(o):
        slot = lax.rem(o, 2)
        span = pl.ds(pl.multiple_of(o * 8, 8), 8)
        return pltpu.make_async_copy(power_hbm.at[:, span], raw.at[slot], raw_sem.at[slot])

    octets = P_SIZE // 8

    for copy in load(0, 0):
        copy.start()
    raw_load(0).start()

    chunks = own // rows

    def first(i, carry):
        slot = lax.rem(i, 2)

        @pl.when(i + 1 < chunks)
        def _():
            for copy in load(i + 1, lax.rem(i + 1, 2)):
                copy.start()

        for copy in load(i, slot):
            copy.wait()

        def eight(g, carry):
            at = i * per + g // 2
            h, rest = at // (2 * groups), lax.rem(at, 2 * groups)
            part, c = rest // groups, lax.rem(rest, groups)
            sub = pl.ds(pl.multiple_of(lax.rem(g, 2) * 8, 8), 8)
            span = pl.ds(pl.multiple_of(g * 8, 8), 8)
            real, imag = [], []
            for n1 in range(P_SIZE):
                lanes = pl.ds(n1 * LANES, LANES)
                d_real, d_imag = mask_entry(code_in[slot, span, lanes])
                x, y = z_in[slot, 0, span, lanes], z_in[slot, 1, span, lanes]
                real.append(d_real * x - d_imag * y)
                imag.append(d_real * y + d_imag * x)
            real, imag = butterflies(real, imag, -1.0)
            for k1 in range(P_SIZE):
                cos, sin = twf_ref[0, k1 : k1 + 1, :], twf_ref[1, k1 : k1 + 1, :]
                buf[k1, h, part, c, sub, 0:LANES] = real[k1] * cos - imag[k1] * sin
                buf[k1, h, part, c, sub, LANES : 2 * LANES] = real[k1] * sin + imag[k1] * cos
            return carry

        return lax.fori_loop(0, rows // 8, eight, carry)

    lax.fori_loop(0, chunks, first, 0)
    greet([{"rows": peer} for peer in peers])

    def span_of(kg):
        return pl.ds(kg * batch, batch)

    def permute(o):
        raw_load(o).wait()

        @pl.when(o + 1 < octets)
        def _():
            raw_load(o + 1).start()

        slot = lax.rem(o, 2)

        def turn(i, carry):
            lanes = pl.ds(pl.multiple_of(i * LANES, LANES), LANES)
            block = raw[slot, :, :, lanes].reshape(Q, LANES)
            turned[pl.ds(pl.multiple_of(i * LANES, LANES), LANES), :] = block.T
            return carry

        lax.fori_loop(0, P_SIZE, turn, 0)

        def back(ak1, carry):
            block = turned[pl.ds(ak1, Q, stride=P_SIZE), :]
            power[o, pl.ds(pl.multiple_of(ak1 * Q, Q), Q), :] = block.T
            return carry

        lax.fori_loop(0, P_SIZE, back, 0)

    def own_copy(kg):
        span = span_of(kg)
        return pltpu.make_async_copy(buf.at[span, :, :, me], got.at[me, span], own_sem.at[kg])

    def send(kg, peer, sender):
        span = span_of(kg)
        return pltpu.make_async_remote_copy(
            src_ref=buf.at[span, :, :, peer],
            dst_ref=got.at[sender, span],
            send_sem=send_sem.at[kg, peer],
            recv_sem=recv_sem.at[kg, sender],
            device_id={"rows": peer},
            device_id_type=MESH,
        )

    def spread(kg):
        def one(j, carry):
            k1 = kg * batch + j
            for h in range(halfs):
                value = buf[k1, h].reshape(2 * Q, 2 * LANES)
                high, low = halves(value)
                dims = ((1,), (1,))
                total = dims_dot(ah_ref[...], high, dims)
                total += dims_dot(ah_ref[...], low, dims)
                total += dims_dot(al_ref[...], high, dims)
                buf[k1, h] = total.reshape(2, groups, share, 2 * LANES)
            return carry

        lax.fori_loop(0, batch, one, 0)
        own_copy(kg).start()
        for peer in peers:
            send(kg, peer, me).start()

    def gather(kg):
        own_copy(kg).wait()
        for peer in peers:
            send(kg, peer, peer).wait_recv()

        def one(j, carry):
            k1 = kg * batch + j
            strided = pl.ds(lax.rem(k1, 8), P_SIZE * share, stride=8)
            weights = power.at[k1 // 8]

            def where(part, h, n1):
                s, tile = n1 // (2 * halfs), n1 % (2 * halfs)
                lanes = pl.ds((tile % 2) * LANES, LANES)
                return s, k1, tile // 2, part, pl.ds(h * 8, 8), lanes

            def fetch(part, h, n1):
                return got[where(part, h, n1)]

            def store(part, h, n1, value):
                got[where(part, h, n1)] = value

            column_block(
                fetch, store, weights, strided, (twf_ref, twi_ref), (fh, fl, ih, il),
                mid_ref, share,
            )
            return carry

        lax.fori_loop(0, batch, one, 0)
        out_copy(kg).start()

    def out_copy(kg):
        span = span_of(kg)
        return pltpu.make_async_copy(got.at[:, span], u_hbm.at[:, span], out_sem.at[kg])

    count = send_sem.shape[0]
    lag = 3

    def turn(i, carry):
        @pl.when(i < count)
        def _():
            spread(i)

        @pl.when(jnp.logical_and(i < count, lax.rem(i * batch, 8) == 0))
        def _():
            permute(i * batch // 8)

        @pl.when(i >= lag)
        def _():
            gather(i - lag)

        return carry

    lax.fori_loop(0, count + lag, turn, 0)

    def finish(kg, carry):
        out_copy(kg).wait()
        for peer in peers:
            send(kg, peer, me).wait_send()
        return carry

    lax.fori_loop(0, count, finish, 0)


def kernel_backward(
    u_hbm, code_hbm, tw_ref, ih, il,
    total_hbm, land_a, land_b, buf, term, code_in, slot, stage,
    code_sem, own_sem, send_sem, recv_sem,
    a_send, a_recv, b_send, b_recv, s_send, s_recv, o_sem, slot_sem,
):
    _, _, _, groups, share, _ = buf.shape
    quarters = send_sem.shape[0]
    chunks, _, tall, _ = land_a.shape
    each = chunks // quarters
    ring = stage.shape[0]
    me, z = lax.axis_index("rows"), lax.axis_index("mask")
    masks = 4
    peers = [lax.rem(me + d, groups) for d in range(1, groups)]
    partner = z + 1 - 2 * lax.rem(z, 2)
    middle = 3 - z
    inner = jnp.logical_or(z == 1, z == 2)
    outer = jnp.logical_or(z == 0, z == 3)

    def place(q):
        return q // 2, pl.ds(pl.multiple_of(lax.rem(q, 2) * LANES, LANES), LANES)

    def own_copy(q):
        h, lanes = place(q)
        return pltpu.make_async_copy(
            u_hbm.at[me, :, h, :, :, lanes], buf.at[:, h, :, me, :, lanes], own_sem.at[q]
        )

    def send(q, peer, sender):
        h, lanes = place(q)
        return pltpu.make_async_remote_copy(
            src_ref=u_hbm.at[peer, :, h, :, :, lanes],
            dst_ref=buf.at[:, h, :, sender, :, lanes],
            send_sem=send_sem.at[q, peer],
            recv_sem=recv_sem.at[q, sender],
            device_id={"rows": peer},
            device_id_type=MESH,
        )

    def code_load(q):
        span = pl.ds(pl.multiple_of(q * LANES, LANES), LANES)
        return pltpu.make_async_copy(code_hbm.at[0, span], code_in.at[lax.rem(q, 2)], code_sem.at[q])

    def start(q):
        code_load(q).start()
        own_copy(q).start()
        for peer in peers:
            send(q, peer, me).start()

    def sent(q):
        for peer in peers:
            send(q, peer, me).wait_send()

    def arrived(q):
        code_load(q).wait()
        own_copy(q).wait()
        for peer in peers:
            send(q, peer, peer).wait_recv()

    def invert(q, least, most):
        h, lanes = place(q)
        span = pl.ds(pl.multiple_of(q * LANES, LANES), LANES)

        def one(k1, carry):
            value = buf[k1, h, :, :, :, lanes].reshape(2 * Q, LANES)
            total = times_table(value.T, ih, il)
            cos, sin = tw_ref[0, pl.ds(k1, 1), :], tw_ref[1, pl.ds(k1, 1), :]
            x, y = total[:, 0:LANES], total[:, LANES : 2 * LANES]
            term[k1, span, 0:LANES] = x * cos - y * sin
            term[k1, span, LANES : 2 * LANES] = x * sin + y * cos
            return carry

        lax.fori_loop(least, most, one, 0)

    def finish(q, least, most):
        def eight(g, carry):
            span = pl.ds(pl.multiple_of(q * LANES + g * 8, 8), 8)
            near = pl.ds(pl.multiple_of(g * 8, 8), 8)
            real = [term[k1, span, 0:LANES] for k1 in range(P_SIZE)]
            imag = [term[k1, span, LANES : 2 * LANES] for k1 in range(P_SIZE)]
            real, imag = butterflies(real, imag, 1.0)
            for n1 in range(P_SIZE):
                code = code_in[lax.rem(q, 2), near, pl.ds(n1 * LANES, LANES)]
                d_real, d_imag = mask_entry(code)
                term[n1, span, 0:LANES] = d_real * real[n1] + d_imag * imag[n1]
                term[n1, span, LANES : 2 * LANES] = d_real * imag[n1] - d_imag * real[n1]
            return carry

        lax.fori_loop(least, most, eight, 0)

    def rows_of(j):
        return pl.ds(pl.multiple_of(j * tall, tall), tall)

    def hop(j, land, send_sems, recv_sems, target):
        return pltpu.make_async_remote_copy(
            src_ref=term.at[:, rows_of(j)],
            dst_ref=land.at[j],
            send_sem=send_sems.at[j],
            recv_sem=recv_sems.at[j],
            device_id={"mask": target},
            device_id_type=MESH,
        )

    def hop_a(j):
        return hop(j, land_a, a_send, a_recv, partner)

    def hop_b(j):
        return hop(j, land_b, b_send, b_recv, middle)

    def hop_s(j):
        return pltpu.make_async_remote_copy(
            src_ref=stage.at[lax.rem(j, ring)],
            dst_ref=total_hbm.at[:, rows_of(j)],
            send_sem=s_send.at[j],
            recv_sem=s_recv.at[j],
            device_id={"mask": partner},
            device_id_type=MESH,
        )

    def keep(j):
        return pltpu.make_async_copy(
            stage.at[lax.rem(j, ring)], total_hbm.at[:, rows_of(j)], o_sem.at[j]
        )

    def outer_step(j):
        @pl.when(j >= 2)
        def _():
            hop_a(j - 2).wait_send()

        hop_a(j).start()

    def inner_first(j):
        hop_a(j).wait_recv()
        copy = pltpu.make_async_copy(land_a.at[j], slot.at[0], slot_sem.at[0])
        copy.start()
        copy.wait()

        def add(n1, carry):
            term[n1, rows_of(j)] = term[n1, rows_of(j)] + slot[0, n1]
            return carry

        lax.fori_loop(0, P_SIZE, add, 0)
        hop_b(j).start()

    def inner_second(j):
        hop_b(j).wait_recv()
        copy = pltpu.make_async_copy(land_b.at[j], slot.at[1], slot_sem.at[1])
        copy.start()

        @pl.when(j >= ring)
        def _():
            hop_s(j - ring).wait_send()
            keep(j - ring).wait()

        copy.wait()
        r = lax.rem(j, ring)
        for n1 in range(P_SIZE):
            lanes = pl.ds(n1 * LANES, LANES)
            total = term[n1, rows_of(j)] + slot[1, n1]
            stage[r, 0, :, lanes] = total[:, 0:LANES]
            stage[r, 1, :, lanes] = total[:, LANES : 2 * LANES]
        hop_s(j).start()
        keep(j).start()

    greet(
        [{"rows": peer} for peer in peers]
        + [{"mask": lax.rem(z + d, masks)} for d in range(1, masks)]
    )
    start(0)
    sent(0)
    start(1)
    arrived(0)
    invert(0, 0, P_SIZE)
    finish(0, 0, LANES // 8)
    half = each // 2
    lines, groups8 = P_SIZE // 2, LANES // 16

    def turn(j, carry):
        q = j // each
        step = lax.rem(j, each) - half

        @pl.when(outer)
        def _():
            outer_step(j)

        @pl.when(inner)
        def _():
            inner_first(j)

            @pl.when(j >= 1)
            def _():
                inner_second(j - 1)

        @pl.when(jnp.logical_and(step == 0, q + 1 < quarters))
        def _():
            arrived(q + 1)

            @pl.when(q + 2 < quarters)
            def _():
                sent(q + 1)
                start(q + 2)

        @pl.when(jnp.logical_and(jnp.logical_and(step >= 0, step < 2), q + 1 < quarters))
        def _():
            invert(q + 1, step * lines, step * lines + lines)

        @pl.when(jnp.logical_and(step >= 2, q + 1 < quarters))
        def _():
            finish(q + 1, (step - 2) * groups8, (step - 1) * groups8)

        return carry

    lax.fori_loop(0, chunks, turn, 0)

    @pl.when(outer)
    def _():
        hop_a(chunks - 2).wait_send()
        hop_a(chunks - 1).wait_send()

        def arrive(j, carry):
            hop_s(j).wait_recv()
            return carry

        lax.fori_loop(0, chunks, arrive, 0)

    @pl.when(inner)
    def _():
        inner_second(chunks - 1)

        def leave(j, carry):
            hop_b(j).wait_send()
            return carry

        lax.fori_loop(0, chunks, leave, 0)

        def last(j, carry):
            hop_s(j).wait_send()
            keep(j).wait()
            return carry

        lax.fori_loop(chunks - ring, chunks, last, 0)

    sent(quarters - 1)


def fast_body(object_field, phases, intensity):
    groups = lax.axis_size("rows")
    masks = lax.axis_size("mask")
    own = object_field.shape[1]
    length = object_field.shape[2]
    share = Q // groups
    half_scale = 1.0 / math.sqrt(length)
    f_high, f_low = host_tables(-1.0, half_scale)
    i_high, i_low = host_tables(1.0, half_scale)
    tw_f, tw_i = host_twiddle(-1.0), host_twiddle(1.0)
    wide = 2 * Q
    f32 = jnp.float32
    vmem = pl.BlockSpec(memory_space=pltpu.VMEM)
    hbm = pl.BlockSpec(memory_space=pl.ANY)
    dma = pltpu.SemaphoreType.DMA

    power = intensity[0].reshape(share, P_SIZE, length)

    parts, rows, halfs = 16, 32, own // wide
    panel = (groups, P_SIZE, halfs, 2, share, wide)
    u = pl.pallas_call(
        kernel_forward,
        in_specs=[hbm] * 3 + [vmem] * 8,
        out_specs=hbm,
        out_shape=jax.ShapeDtypeStruct(panel, f32),
        scratch_shapes=[
            pltpu.VMEM((P_SIZE, halfs, 2, groups, share, wide), f32),
            pltpu.VMEM(panel, f32),
            pltpu.VMEM((2, 2, rows, length), f32),
            pltpu.VMEM((2, rows, length), jnp.int32),
            pltpu.VMEM((2, share, 8, length), f32),
            pltpu.VMEM((length, 8 * share), f32),
            pltpu.VMEM((P_SIZE // 8, length, Q), f32),
            pltpu.VMEM((P_SIZE * share, wide), f32),
            dma((2,)),
            dma((2,)),
            dma((2,)),
            dma((parts,)),
            dma((parts,)),
            dma((parts, groups)),
            dma((parts, groups)),
        ],
        compiler_params=pltpu.CompilerParams(
            collective_id=0, has_side_effects=True, vmem_limit_bytes=58 * 2**20
        ),
        name="forward_and_columns",
    )(object_field, phases, power, tw_f, tw_i, f_high.T, f_low.T, f_high, f_low, i_high, i_low)

    quarters, tall, ring = own // LANES, 16, 4
    chunks = own // tall
    landing = jax.ShapeDtypeStruct((chunks, P_SIZE, tall, wide), f32)
    total, _, _ = pl.pallas_call(
        kernel_backward,
        in_specs=[hbm] * 2 + [vmem] * 3,
        out_specs=[hbm] * 3,
        out_shape=[jax.ShapeDtypeStruct((2, own, length), f32), landing, landing],
        scratch_shapes=[
            pltpu.VMEM((P_SIZE, halfs, 2, groups, share, wide), f32),
            pltpu.VMEM((P_SIZE, own, wide), f32),
            pltpu.VMEM((2, LANES, length), jnp.int32),
            pltpu.VMEM((2, P_SIZE, tall, wide), f32),
            pltpu.VMEM((ring, 2, tall, length), f32),
            dma((quarters,)),
            dma((quarters,)),
            dma((quarters, groups)),
            dma((quarters, groups)),
        ]
        + [dma((chunks,))] * 7
        + [dma((2,))],
        compiler_params=pltpu.CompilerParams(
            collective_id=1, has_side_effects=True, vmem_limit_bytes=58 * 2**20
        ),
        name="back_and_sum",
    )(u, phases, tw_i, i_high, i_low)
    direction = total * (1.0 / masks)
    return (object_field - step_size * direction, direction)


def solution(mesh):
    def body(object_field, phases, intensity):
        groups = lax.axis_size("rows")
        masks = lax.axis_size("mask")
        own, length = object_field.shape[1:]
        fits = own % LANES == 0 and length == P_SIZE * Q and groups == 8 and masks == 4 and own % 256 == 0
        run = fast_body if fits else plain_body
        return run(object_field, phases, intensity)

    return jax.shard_map(
        body,
        mesh=mesh,
        in_specs=(P(None, "rows", None), P("mask", "rows", None), P("mask", "rows", None)),
        out_specs=(P(None, "rows", None), P(None, "rows", None)),
        check_vma=False,
    )
```

```python
import math

import jax
import jax.numpy as jnp
import ml_dtypes
import numpy as np
from jax import lax
from jax.experimental import pallas as pl
from jax.experimental.pallas import tpu as pltpu
from jax.sharding import PartitionSpec as P

P_SIZE = 32
Q = 128


step_size = 0.2


def dft_table(length, sign):
    idx = jnp.arange(length, dtype=jnp.int32)
    expo = idx[:, None] * idx[None, :] % length
    angle = expo.astype(jnp.float32) * (sign * 2.0 * math.pi / length)
    return (jnp.cos(angle), jnp.sin(angle))


def twiddle_table(first, second, sign):
    left = jnp.arange(first, dtype=jnp.int32)
    right = jnp.arange(second, dtype=jnp.int32)
    total = first * second
    expo = left[:, None] * right[None, :] % total
    angle = expo.astype(jnp.float32) * (sign * 2.0 * math.pi / total)
    return (jnp.cos(angle), jnp.sin(angle))


def stacked_table(t_real, t_imag):
    upper = jnp.stack([t_real, t_imag], axis=1)
    lower = jnp.stack([-t_imag, t_real], axis=1)
    return jnp.stack([upper, lower])


def contract(form, left, right):
    return jnp.einsum(
        form, left, right, precision=lax.Precision.HIGHEST, preferred_element_type=jnp.float32
    )


def along_last(stacked, sign, flip):
    lead = stacked.shape[1]
    length = P_SIZE * Q
    p_real, p_imag = dft_table(P_SIZE, sign)
    q_real, q_imag = dft_table(Q, sign)
    t_real, t_imag = twiddle_table(P_SIZE, Q, sign)
    factor = 1.0 / math.sqrt(length)
    first_table = stacked_table(p_real, p_imag)
    second_table = stacked_table(q_real * factor, q_imag * factor)
    inner = contract("cbpq,cpek->ebkq", stacked.reshape(2, lead, P_SIZE, Q), first_table)
    b_real = inner[0] * t_real - inner[1] * t_imag
    b_imag = inner[0] * t_imag + inner[1] * t_real
    twisted = jnp.stack([b_real, b_imag])
    if flip:
        return contract("cbkq,cqem->emkb", twisted, second_table).reshape(2, length, lead)
    return contract("cbkq,cqem->ebmk", twisted, second_table).reshape(2, lead, length)


def plain_body(object_field, phases, intensity):
    groups = lax.axis_size("rows")
    masks = lax.axis_size("mask")
    own_rows = object_field.shape[1]
    length = object_field.shape[2]
    own_cols = length // groups
    code = phases[0]
    d_real = jnp.where(code == 0, 1.0, 0.0) - jnp.where(code == 2, 1.0, 0.0)
    d_imag = jnp.where(code == 1, 1.0, 0.0) - jnp.where(code == 3, 1.0, 0.0)
    z_real = object_field[0]
    z_imag = object_field[1]
    coded = jnp.stack([d_real * z_real - d_imag * z_imag, d_real * z_imag + d_imag * z_real])
    result = along_last(coded, -1.0, True)
    received = lax.all_to_all(
        result.reshape(2, groups, own_cols, own_rows),
        "rows",
        split_axis=1,
        concat_axis=1,
        tiled=True,
    )
    columns = jnp.transpose(received, (0, 2, 1, 3)).reshape(2, own_cols, length)
    wave = along_last(columns, -1.0, False)
    weight = wave[0] * wave[0] + wave[1] * wave[1] - intensity[0]
    weighted = along_last(wave * weight[None], 1.0, False)
    outgoing = weighted.reshape(2, own_cols, groups, own_rows)
    returned = lax.all_to_all(outgoing, "rows", split_axis=2, concat_axis=2, tiled=True)
    panel = jnp.transpose(returned, (0, 3, 2, 1)).reshape(2, own_rows, length)
    back = along_last(panel, 1.0, False)
    g_real = back[0]
    g_imag = back[1]
    term = jnp.stack([d_real * g_real + d_imag * g_imag, d_real * g_imag - d_imag * g_real])
    inverse_count = 1.0 / masks
    total = lax.psum(term, "mask")
    direction = inverse_count * total
    return (object_field - step_size * direction, direction)


LANES = 128


def host_tables(sign, scale):
    idx = np.arange(Q)
    angle = sign * 2.0 * np.pi * ((idx[:, None] * idx[None, :]) % Q) / Q
    cos, sin = np.cos(angle) * scale, np.sin(angle) * scale
    table = np.block([[cos, sin], [-sin, cos]]).astype(np.float32)
    high = table.astype(ml_dtypes.bfloat16)
    low = (table - high.astype(np.float32)).astype(ml_dtypes.bfloat16)
    return high, low


def host_twiddle(sign):
    expo = np.arange(P_SIZE)[:, None] * np.arange(Q)[None, :]
    angle = sign * 2.0 * np.pi * expo / (P_SIZE * Q)
    return np.stack([np.cos(angle), np.sin(angle)]).astype(np.float32)


def butterflies(real, imag, sign):
    count = len(real)
    if count == 1:
        return real, imag
    e_real, e_imag = butterflies(real[0::2], imag[0::2], sign)
    o_real, o_imag = butterflies(real[1::2], imag[1::2], sign)
    half = count // 2
    out_real, out_imag = [None] * count, [None] * count
    for k in range(half):
        a, b = o_real[k], o_imag[k]
        if k == 0:
            t_real, t_imag = a, b
        elif 4 * k == count:
            t_real, t_imag = (b, -a) if sign < 0 else (-b, a)
        elif 8 * k == count:
            root = math.sqrt(0.5)
            if sign < 0:
                t_real, t_imag = (a + b) * root, (b - a) * root
            else:
                t_real, t_imag = (a - b) * root, (a + b) * root
        elif 8 * k == 3 * count:
            root = math.sqrt(0.5)
            if sign < 0:
                t_real, t_imag = (b - a) * root, (a + b) * -root
            else:
                t_real, t_imag = (a + b) * -root, (a - b) * root
        else:
            angle = sign * 2.0 * math.pi * k / count
            c, s = math.cos(angle), math.sin(angle)
            t_real, t_imag = a * c - b * s, a * s + b * c
        out_real[k], out_imag[k] = e_real[k] + t_real, e_imag[k] + t_imag
        out_real[k + half], out_imag[k + half] = e_real[k] - t_real, e_imag[k] - t_imag
    return out_real, out_imag


def halves(value):
    high = value.astype(jnp.bfloat16)
    low = (value - high.astype(jnp.float32)).astype(jnp.bfloat16)
    return high, low


def dims_dot(left, right, dims):
    return lax.dot_general(left, right, (dims, ((), ())), preferred_element_type=jnp.float32)


def times_table(value, high_ref, low_ref):
    high, low = halves(value)
    dims = ((1,), (0,))
    total = dims_dot(high, high_ref[...], dims)
    total += dims_dot(low, high_ref[...], dims)
    return total + dims_dot(high, low_ref[...], dims)


def mask_entry(code):
    d_real = jnp.where(code == 0, 1.0, 0.0) - jnp.where(code == 2, 1.0, 0.0)
    d_imag = jnp.where(code == 1, 1.0, 0.0) - jnp.where(code == 3, 1.0, 0.0)
    return d_real, d_imag


def column_block(load, store, power_ref, power_rows, tw_refs, tables, mid_ref, share):
    twf_ref, twi_ref = tw_refs
    fh_ref, fl_ref, ih_ref, il_ref = tables
    for h in range(share // 8):
        real = [load(0, h, n1) for n1 in range(P_SIZE)]
        imag = [load(1, h, n1) for n1 in range(P_SIZE)]
        real, imag = butterflies(real, imag, -1.0)
        for k1 in range(P_SIZE):
            c, s = twf_ref[0, k1 : k1 + 1, :], twf_ref[1, k1 : k1 + 1, :]
            at = slice(k1 * share + h * 8, k1 * share + h * 8 + 8)
            mid_ref[at, 0:LANES] = real[k1] * c - imag[k1] * s
            mid_ref[at, LANES : 2 * LANES] = real[k1] * s + imag[k1] * c
    wave = times_table(mid_ref[...], fh_ref, fl_ref)
    w_real, w_imag = wave[:, 0:LANES], wave[:, LANES : 2 * LANES]
    weight = w_real * w_real + w_imag * w_imag - power_ref[power_rows, :]
    value = jnp.concatenate([w_real * weight, w_imag * weight], axis=1)
    mid_ref[...] = times_table(value, ih_ref, il_ref)
    for h in range(share // 8):
        real, imag = [], []
        for k1 in range(P_SIZE):
            c, s = twi_ref[0, k1 : k1 + 1, :], twi_ref[1, k1 : k1 + 1, :]
            at = slice(k1 * share + h * 8, k1 * share + h * 8 + 8)
            x, y = mid_ref[at, 0:LANES], mid_ref[at, LANES : 2 * LANES]
            real.append(x * c - y * s)
            imag.append(x * s + y * c)
        real, imag = butterflies(real, imag, 1.0)
        for n1 in range(P_SIZE):
            store(0, h, n1, real[n1])
            store(1, h, n1, imag[n1])


MESH = pl.DeviceIdType.MESH


def greet(peers):
    barrier = pltpu.get_barrier_semaphore()
    for peer in peers:
        pl.semaphore_signal(barrier, inc=1, device_id=peer, device_id_type=MESH)
    pl.semaphore_wait(barrier, len(peers))


def kernel_forward(
    z_hbm, code_hbm, power_hbm, twf_ref, twi_ref, ah_ref, al_ref, fh, fl, ih, il,
    u_hbm, buf, got, z_in, code_in, raw, turned, power, mid_ref,
    z_sem, code_sem, raw_sem, own_sem, out_sem, send_sem, recv_sem,
):
    _, halfs, _, groups, share, _ = buf.shape
    rows = z_in.shape[2]
    own = z_hbm.shape[1]
    batch = P_SIZE // send_sem.shape[0]
    per = rows // share
    me = lax.axis_index("rows")
    peers = [lax.rem(me + d, groups) for d in range(1, groups)]

    def load(i, slot):
        span = pl.ds(pl.multiple_of(i * rows, rows), rows)
        return (
            pltpu.make_async_copy(z_hbm.at[:, span], z_in.at[slot], z_sem.at[slot]),
            pltpu.make_async_copy(code_hbm.at[0, span], code_in.at[slot], code_sem.at[slot]),
        )

    def raw_load(o):
        slot = lax.rem(o, 2)
        span = pl.ds(pl.multiple_of(o * 8, 8), 8)
        return pltpu.make_async_copy(power_hbm.at[:, span], raw.at[slot], raw_sem.at[slot])

    octets = P_SIZE // 8

    for copy in load(0, 0):
        copy.start()
    raw_load(0).start()

    chunks = own // rows

    def first(i, carry):
        slot = lax.rem(i, 2)

        @pl.when(i + 1 < chunks)
        def _():
            for copy in load(i + 1, lax.rem(i + 1, 2)):
                copy.start()

        for copy in load(i, slot):
            copy.wait()

        def eight(g, carry):
            at = i * per + g // 2
            h, rest = at // (2 * groups), lax.rem(at, 2 * groups)
            part, c = rest // groups, lax.rem(rest, groups)
            sub = pl.ds(pl.multiple_of(lax.rem(g, 2) * 8, 8), 8)
            span = pl.ds(pl.multiple_of(g * 8, 8), 8)
            real, imag = [], []
            for n1 in range(P_SIZE):
                lanes = pl.ds(n1 * LANES, LANES)
                d_real, d_imag = mask_entry(code_in[slot, span, lanes])
                x, y = z_in[slot, 0, span, lanes], z_in[slot, 1, span, lanes]
                real.append(d_real * x - d_imag * y)
                imag.append(d_real * y + d_imag * x)
            real, imag = butterflies(real, imag, -1.0)
            for k1 in range(P_SIZE):
                cos, sin = twf_ref[0, k1 : k1 + 1, :], twf_ref[1, k1 : k1 + 1, :]
                buf[k1, h, part, c, sub, 0:LANES] = real[k1] * cos - imag[k1] * sin
                buf[k1, h, part, c, sub, LANES : 2 * LANES] = real[k1] * sin + imag[k1] * cos
            return carry

        return lax.fori_loop(0, rows // 8, eight, carry)

    lax.fori_loop(0, chunks, first, 0)
    greet([{"rows": peer} for peer in peers])

    def span_of(kg):
        return pl.ds(kg * batch, batch)

    def permute(o):
        raw_load(o).wait()

        @pl.when(o + 1 < octets)
        def _():
            raw_load(o + 1).start()

        slot = lax.rem(o, 2)

        def turn(i, carry):
            lanes = pl.ds(pl.multiple_of(i * LANES, LANES), LANES)
            block = raw[slot, :, :, lanes].reshape(Q, LANES)
            turned[pl.ds(pl.multiple_of(i * LANES, LANES), LANES), :] = block.T
            return carry

        lax.fori_loop(0, P_SIZE, turn, 0)

        def back(ak1, carry):
            block = turned[pl.ds(ak1, Q, stride=P_SIZE), :]
            power[o, pl.ds(pl.multiple_of(ak1 * Q, Q), Q), :] = block.T
            return carry

        lax.fori_loop(0, P_SIZE, back, 0)

    def own_copy(kg):
        span = span_of(kg)
        return pltpu.make_async_copy(buf.at[span, :, :, me], got.at[me, span], own_sem.at[kg])

    def send(kg, peer, sender):
        span = span_of(kg)
        return pltpu.make_async_remote_copy(
            src_ref=buf.at[span, :, :, peer],
            dst_ref=got.at[sender, span],
            send_sem=send_sem.at[kg, peer],
            recv_sem=recv_sem.at[kg, sender],
            device_id={"rows": peer},
            device_id_type=MESH,
        )

    def spread(kg):
        def one(j, carry):
            k1 = kg * batch + j
            for h in range(halfs):
                value = buf[k1, h].reshape(2 * Q, 2 * LANES)
                high, low = halves(value)
                dims = ((1,), (1,))
                total = dims_dot(ah_ref[...], high, dims)
                total += dims_dot(ah_ref[...], low, dims)
                total += dims_dot(al_ref[...], high, dims)
                buf[k1, h] = total.reshape(2, groups, share, 2 * LANES)
            return carry

        lax.fori_loop(0, batch, one, 0)
        own_copy(kg).start()
        for peer in peers:
            send(kg, peer, me).start()

    def gather(kg):
        own_copy(kg).wait()
        for peer in peers:
            send(kg, peer, peer).wait_recv()

        def one(j, carry):
            k1 = kg * batch + j
            strided = pl.ds(lax.rem(k1, 8), P_SIZE * share, stride=8)
            weights = power.at[k1 // 8]

            def where(part, h, n1):
                s, tile = n1 // (2 * halfs), n1 % (2 * halfs)
                lanes = pl.ds((tile % 2) * LANES, LANES)
                return s, k1, tile // 2, part, pl.ds(h * 8, 8), lanes

            def fetch(part, h, n1):
                return got[where(part, h, n1)]

            def store(part, h, n1, value):
                got[where(part, h, n1)] = value

            column_block(
                fetch, store, weights, strided, (twf_ref, twi_ref), (fh, fl, ih, il),
                mid_ref, share,
            )
            return carry

        lax.fori_loop(0, batch, one, 0)
        out_copy(kg).start()

    def out_copy(kg):
        span = span_of(kg)
        return pltpu.make_async_copy(got.at[:, span], u_hbm.at[:, span], out_sem.at[kg])

    count = send_sem.shape[0]
    lag = 3

    def turn(i, carry):
        @pl.when(i < count)
        def _():
            spread(i)

        @pl.when(jnp.logical_and(i < count, lax.rem(i * batch, 8) == 0))
        def _():
            permute(i * batch // 8)

        @pl.when(i >= lag)
        def _():
            gather(i - lag)

        return carry

    lax.fori_loop(0, count + lag, turn, 0)

    def finish(kg, carry):
        out_copy(kg).wait()
        for peer in peers:
            send(kg, peer, me).wait_send()
        return carry

    lax.fori_loop(0, count, finish, 0)


def kernel_backward(
    u_hbm, code_hbm, tw_ref, ih, il,
    total_hbm, land_a, land_b, buf, term, code_in, slot, stage,
    code_sem, own_sem, send_sem, recv_sem,
    a_send, a_recv, b_send, b_recv, s_send, s_recv, o_sem, slot_sem,
):
    _, _, _, groups, share, _ = buf.shape
    quarters = send_sem.shape[0]
    chunks, _, tall, _ = land_a.shape
    each = chunks // quarters
    ring = stage.shape[0]
    me, z = lax.axis_index("rows"), lax.axis_index("mask")
    masks = 4
    peers = [lax.rem(me + d, groups) for d in range(1, groups)]
    partner = z + 1 - 2 * lax.rem(z, 2)
    middle = 3 - z
    inner = jnp.logical_or(z == 1, z == 2)
    outer = jnp.logical_or(z == 0, z == 3)

    def place(q):
        return q // 2, pl.ds(pl.multiple_of(lax.rem(q, 2) * LANES, LANES), LANES)

    def own_copy(q):
        h, lanes = place(q)
        return pltpu.make_async_copy(
            u_hbm.at[me, :, h, :, :, lanes], buf.at[:, h, :, me, :, lanes], own_sem.at[q]
        )

    def send(q, peer, sender):
        h, lanes = place(q)
        return pltpu.make_async_remote_copy(
            src_ref=u_hbm.at[peer, :, h, :, :, lanes],
            dst_ref=buf.at[:, h, :, sender, :, lanes],
            send_sem=send_sem.at[q, peer],
            recv_sem=recv_sem.at[q, sender],
            device_id={"rows": peer},
            device_id_type=MESH,
        )

    def code_load(q):
        span = pl.ds(pl.multiple_of(q * LANES, LANES), LANES)
        return pltpu.make_async_copy(code_hbm.at[0, span], code_in.at[lax.rem(q, 2)], code_sem.at[q])

    def start(q):
        code_load(q).start()
        own_copy(q).start()
        for peer in peers:
            send(q, peer, me).start()

    def sent(q):
        for peer in peers:
            send(q, peer, me).wait_send()

    def arrived(q):
        code_load(q).wait()
        own_copy(q).wait()
        for peer in peers:
            send(q, peer, peer).wait_recv()

    def invert(q, least, most):
        h, lanes = place(q)
        span = pl.ds(pl.multiple_of(q * LANES, LANES), LANES)

        def one(k1, carry):
            value = buf[k1, h, :, :, :, lanes].reshape(2 * Q, LANES)
            total = times_table(value.T, ih, il)
            cos, sin = tw_ref[0, pl.ds(k1, 1), :], tw_ref[1, pl.ds(k1, 1), :]
            x, y = total[:, 0:LANES], total[:, LANES : 2 * LANES]
            term[k1, span, 0:LANES] = x * cos - y * sin
            term[k1, span, LANES : 2 * LANES] = x * sin + y * cos
            return carry

        lax.fori_loop(least, most, one, 0)

    def finish(q, least, most):
        def eight(g, carry):
            span = pl.ds(pl.multiple_of(q * LANES + g * 8, 8), 8)
            near = pl.ds(pl.multiple_of(g * 8, 8), 8)
            real = [term[k1, span, 0:LANES] for k1 in range(P_SIZE)]
            imag = [term[k1, span, LANES : 2 * LANES] for k1 in range(P_SIZE)]
            real, imag = butterflies(real, imag, 1.0)
            for n1 in range(P_SIZE):
                code = code_in[lax.rem(q, 2), near, pl.ds(n1 * LANES, LANES)]
                d_real, d_imag = mask_entry(code)
                term[n1, span, 0:LANES] = d_real * real[n1] + d_imag * imag[n1]
                term[n1, span, LANES : 2 * LANES] = d_real * imag[n1] - d_imag * real[n1]
            return carry

        lax.fori_loop(least, most, eight, 0)

    def rows_of(j):
        return pl.ds(pl.multiple_of(j * tall, tall), tall)

    def hop(j, land, send_sems, recv_sems, target):
        return pltpu.make_async_remote_copy(
            src_ref=term.at[:, rows_of(j)],
            dst_ref=land.at[j],
            send_sem=send_sems.at[j],
            recv_sem=recv_sems.at[j],
            device_id={"mask": target},
            device_id_type=MESH,
        )

    def hop_a(j):
        return hop(j, land_a, a_send, a_recv, partner)

    def hop_b(j):
        return hop(j, land_b, b_send, b_recv, middle)

    def hop_s(j):
        return pltpu.make_async_remote_copy(
            src_ref=stage.at[lax.rem(j, ring)],
            dst_ref=total_hbm.at[:, rows_of(j)],
            send_sem=s_send.at[j],
            recv_sem=s_recv.at[j],
            device_id={"mask": partner},
            device_id_type=MESH,
        )

    def keep(j):
        return pltpu.make_async_copy(
            stage.at[lax.rem(j, ring)], total_hbm.at[:, rows_of(j)], o_sem.at[j]
        )

    def outer_step(j):
        @pl.when(j >= 2)
        def _():
            hop_a(j - 2).wait_send()

        hop_a(j).start()

    def inner_first(j):
        hop_a(j).wait_recv()
        copy = pltpu.make_async_copy(land_a.at[j], slot.at[0], slot_sem.at[0])
        copy.start()
        copy.wait()

        def add(n1, carry):
            term[n1, rows_of(j)] = term[n1, rows_of(j)] + slot[0, n1]
            return carry

        lax.fori_loop(0, P_SIZE, add, 0)
        hop_b(j).start()

    def inner_second(j):
        hop_b(j).wait_recv()
        copy = pltpu.make_async_copy(land_b.at[j], slot.at[1], slot_sem.at[1])
        copy.start()

        @pl.when(j >= ring)
        def _():
            hop_s(j - ring).wait_send()
            keep(j - ring).wait()

        copy.wait()
        r = lax.rem(j, ring)
        for n1 in range(P_SIZE):
            lanes = pl.ds(n1 * LANES, LANES)
            total = term[n1, rows_of(j)] + slot[1, n1]
            stage[r, 0, :, lanes] = total[:, 0:LANES]
            stage[r, 1, :, lanes] = total[:, LANES : 2 * LANES]
        hop_s(j).start()
        keep(j).start()

    greet(
        [{"rows": peer} for peer in peers]
        + [{"mask": lax.rem(z + d, masks)} for d in range(1, masks)]
    )
    start(0)
    sent(0)
    start(1)
    arrived(0)
    invert(0, 0, P_SIZE)
    finish(0, 0, LANES // 8)
    half = each // 2
    pieces = half // 2
    lines, groups8 = P_SIZE // pieces, LANES // 8 // pieces

    def turn(j, carry):
        q = j // each
        step = lax.rem(j, each) - half

        @pl.when(outer)
        def _():
            outer_step(j)

        @pl.when(inner)
        def _():
            inner_first(j)

            @pl.when(j >= 1)
            def _():
                inner_second(j - 1)

        @pl.when(jnp.logical_and(step == 0, q + 1 < quarters))
        def _():
            arrived(q + 1)

            @pl.when(q + 2 < quarters)
            def _():
                sent(q + 1)
                start(q + 2)

        @pl.when(jnp.logical_and(jnp.logical_and(step >= 0, step < pieces), q + 1 < quarters))
        def _():
            invert(q + 1, step * lines, step * lines + lines)

        @pl.when(jnp.logical_and(step >= pieces, q + 1 < quarters))
        def _():
            finish(q + 1, (step - pieces) * groups8, (step - pieces + 1) * groups8)

        return carry

    lax.fori_loop(0, chunks, turn, 0)

    @pl.when(outer)
    def _():
        hop_a(chunks - 2).wait_send()
        hop_a(chunks - 1).wait_send()

        def arrive(j, carry):
            hop_s(j).wait_recv()
            return carry

        lax.fori_loop(0, chunks, arrive, 0)

    @pl.when(inner)
    def _():
        inner_second(chunks - 1)

        def leave(j, carry):
            hop_b(j).wait_send()
            return carry

        lax.fori_loop(0, chunks, leave, 0)

        def last(j, carry):
            hop_s(j).wait_send()
            keep(j).wait()
            return carry

        lax.fori_loop(chunks - ring, chunks, last, 0)

    sent(quarters - 1)


def fast_body(object_field, phases, intensity):
    groups = lax.axis_size("rows")
    masks = lax.axis_size("mask")
    own = object_field.shape[1]
    length = object_field.shape[2]
    share = Q // groups
    half_scale = 1.0 / math.sqrt(length)
    f_high, f_low = host_tables(-1.0, half_scale)
    i_high, i_low = host_tables(1.0, half_scale)
    tw_f, tw_i = host_twiddle(-1.0), host_twiddle(1.0)
    wide = 2 * Q
    f32 = jnp.float32
    vmem = pl.BlockSpec(memory_space=pltpu.VMEM)
    hbm = pl.BlockSpec(memory_space=pl.ANY)
    dma = pltpu.SemaphoreType.DMA

    power = intensity[0].reshape(share, P_SIZE, length)

    parts, rows, halfs = 16, 32, own // wide
    panel = (groups, P_SIZE, halfs, 2, share, wide)
    u = pl.pallas_call(
        kernel_forward,
        in_specs=[hbm] * 3 + [vmem] * 8,
        out_specs=hbm,
        out_shape=jax.ShapeDtypeStruct(panel, f32),
        scratch_shapes=[
            pltpu.VMEM((P_SIZE, halfs, 2, groups, share, wide), f32),
            pltpu.VMEM(panel, f32),
            pltpu.VMEM((2, 2, rows, length), f32),
            pltpu.VMEM((2, rows, length), jnp.int32),
            pltpu.VMEM((2, share, 8, length), f32),
            pltpu.VMEM((length, 8 * share), f32),
            pltpu.VMEM((P_SIZE // 8, length, Q), f32),
            pltpu.VMEM((P_SIZE * share, wide), f32),
            dma((2,)),
            dma((2,)),
            dma((2,)),
            dma((parts,)),
            dma((parts,)),
            dma((parts, groups)),
            dma((parts, groups)),
        ],
        compiler_params=pltpu.CompilerParams(
            collective_id=0, has_side_effects=True, vmem_limit_bytes=58 * 2**20
        ),
        name="forward_and_columns",
    )(object_field, phases, power, tw_f, tw_i, f_high.T, f_low.T, f_high, f_low, i_high, i_low)

    quarters, tall, ring = own // LANES, 8, 4
    chunks = own // tall
    landing = jax.ShapeDtypeStruct((chunks, P_SIZE, tall, wide), f32)
    total, _, _ = pl.pallas_call(
        kernel_backward,
        in_specs=[hbm] * 2 + [vmem] * 3,
        out_specs=[hbm] * 3,
        out_shape=[jax.ShapeDtypeStruct((2, own, length), f32), landing, landing],
        scratch_shapes=[
            pltpu.VMEM((P_SIZE, halfs, 2, groups, share, wide), f32),
            pltpu.VMEM((P_SIZE, own, wide), f32),
            pltpu.VMEM((2, LANES, length), jnp.int32),
            pltpu.VMEM((2, P_SIZE, tall, wide), f32),
            pltpu.VMEM((ring, 2, tall, length), f32),
            dma((quarters,)),
            dma((quarters,)),
            dma((quarters, groups)),
            dma((quarters, groups)),
        ]
        + [dma((chunks,))] * 7
        + [dma((2,))],
        compiler_params=pltpu.CompilerParams(
            collective_id=1, has_side_effects=True, vmem_limit_bytes=58 * 2**20
        ),
        name="back_and_sum",
    )(u, phases, tw_i, i_high, i_low)
    direction = total * (1.0 / masks)
    return (object_field - step_size * direction, direction)


def solution(mesh):
    def body(object_field, phases, intensity):
        groups = lax.axis_size("rows")
        masks = lax.axis_size("mask")
        own, length = object_field.shape[1:]
        fits = own % LANES == 0 and length == P_SIZE * Q and groups == 8 and masks == 4 and own % 256 == 0
        run = fast_body if fits else plain_body
        return run(object_field, phases, intensity)

    return jax.shard_map(
        body,
        mesh=mesh,
        in_specs=(P(None, "rows", None), P("mask", "rows", None), P("mask", "rows", None)),
        out_specs=(P(None, "rows", None), P(None, "rows", None)),
        check_vma=False,
    )
```
